256 devices in a mesh: samp: 32 (over z, y), rows: 8 (over x, core).
Axes of the slice: x: 4, y: 4, z: 8, core: 2. Of those that a mesh axis runs over, the one named last changes fastest.
Arguments:
- samples: float32 [32, 640, 4480], P('samp', 'rows'), may hold values from -6 to 6
- truth_field: float32 [640, 4480], P('rows', 'samp'), may hold values from -6 to 6
Outputs:
- contrast_fine: float32 [32, 640, 4480], P('samp', 'rows')
- contrast_half: float32 [32, 320, 2240], P('samp', 'rows')
- contrast_quarter: float32 [32, 160, 1120], P('samp', 'rows')
- contrast_eighth: float32 [32, 80, 560], P('samp', 'rows')
- similarity_coarse: float32 [32, 40, 280], P('samp', 'rows')
The draws below stay inside these ranges and needn't reach their ends.
All inputs are finite; a program needn't handle non-finite values.
Results may differ from the reference program's by a relative error of at most 0.00002.
Values sent between devices are 32-bit elements; how exact they have to be, the bound alone decides.
No kernel may reach another device: no remote copies, remote signals or barrier semaphores. Data moves between devices by JAX's collectives and lax.ppermute only.
A program may use at most 128 MiB of HBM per device.

```python
import jax
import jax.numpy as jnp
from jax import lax

COLS = 4480
SAMPLES = 32
HEIGHT = 640


def shard_levels(stream_key, dims, pieces, least, high):
    factor_of = 1.0
    for axis_at, blocks in pieces:
        heights = jax.random.uniform(jax.random.fold_in(jax.random.fold_in(stream_key, 6), axis_at), (blocks,), jnp.float32, least / len(pieces), high / len(pieces))
        factor_of = factor_of * jnp.repeat(jnp.exp(heights), dims[axis_at] // blocks).reshape((-1,) + (1,) * (len(dims) - 1 - axis_at))
    return factor_of


def scatter_about(key, extent, deviation, bound, cuts=(), held_as=jnp.bfloat16):
    drawn = deviation * jax.random.normal(key, extent, jnp.float32)
    if cuts:
        drawn = drawn * shard_levels(key, extent, cuts, -0.22, 0.18)
    return jnp.clip(drawn, -bound, bound).astype(held_as)


def setup_inputs(seed: int = 0) -> dict:
    key_of = jax.random.split(jax.random.key(seed), 3)
    return {
        "samples": scatter_about(key_of[0], (SAMPLES, HEIGHT, COLS), 1.0, 6.0, ((0, 32), (1, 8)), jnp.float32),
        "truth_field": scatter_about(key_of[1], (HEIGHT, COLS), 1.0, 6.0, ((0, 8), (1, 32)), jnp.float32),
    }


small_one = 1e-4
small_two = 9e-4


def window():
    offsets = jnp.arange(11).astype(jnp.float32) - 5.0
    shaped = jnp.exp(-offsets * offsets / 4.5)
    return shaped / jnp.sum(shaped)


def smooth(padded, weights):
    row_count = padded.shape[-2] - 10
    column_count = padded.shape[-1]
    vertical = weights[0] * padded[..., 0:row_count, :]
    for tap_index in range(1, 11):
        vertical = vertical + weights[tap_index] * padded[..., tap_index:tap_index + row_count, :]
    widths = [(0, 0)] * (padded.ndim - 1) + [(5, 5)]
    widened = jnp.pad(vertical, widths)
    result = weights[0] * widened[..., 0:column_count]
    for tap_index in range(1, 11):
        result = result + weights[tap_index] * widened[..., tap_index:tap_index + column_count]
    return result


def halve_grid(field):
    leading = field.shape[:-2]
    row_count = field.shape[-2]
    column_count = field.shape[-1]
    blocks = field.reshape(leading + (row_count // 2, 2, column_count // 2, 2))
    return 0.25 * (blocks[..., 0, :, 0] + blocks[..., 0, :, 1] + blocks[..., 1, :, 0] + blocks[..., 1, :, 1])


def level_maps(sample_pad, truth_pad, weights, coarsest):
    mean_x = smooth(sample_pad, weights)
    mean_y = smooth(truth_pad, weights)
    second_x = smooth(sample_pad * sample_pad, weights)
    second_y = smooth(truth_pad * truth_pad, weights)
    cross_xy = smooth(sample_pad * truth_pad, weights)
    var_x = second_x - mean_x * mean_x
    var_y = second_y - mean_y * mean_y
    covar = cross_xy - mean_x * mean_y
    contrast = (2.0 * covar + small_two) / (var_x + var_y + small_two)
    if coarsest:
        luminance = (2.0 * mean_x * mean_y + small_one) / (mean_x * mean_x + mean_y * mean_y + small_one)
        return luminance * contrast
    return contrast


def reference(samples, truth_field):
    weights = window()
    truth_levels = [truth_field]
    for level_index in range(1, 5):
        truth_levels.append(halve_grid(truth_levels[-1]))
    rim_widths = [(5, 5), (0, 0)]

    def one_sample(field):
        results = []
        current = field
        for level_index in range(5):
            if level_index > 0:
                current = halve_grid(current)
            results.append(level_maps(jnp.pad(current, rim_widths), jnp.pad(truth_levels[level_index], rim_widths), weights, level_index == 4))
        return tuple(results)

    mapped = lax.map(one_sample, samples)
    return (mapped[0], mapped[1], mapped[2], mapped[3], mapped[4])
```

```python
import functools

import jax
import jax.numpy as jnp
import numpy as np
from jax import lax
from jax.experimental import pallas as pl
from jax.experimental.pallas import tpu as pltpu
from jax.sharding import PartitionSpec as P

small_one = 0.0001
small_two = 0.0009

ROWS = (80, 40, 20, 10, 5)
COLS = (4480, 2240, 1120, 560, 280)
TILES = tuple(-(-c // 128) for c in COLS)
STRIPS = tuple(t + 1 for t in TILES)
HELD = (80, 48, 32, 16, 8)
POOLED = (80, 40, 24, 16, 8)
WORK = (80, 48, 32, 16, 16)
EDGE_AT = tuple(int(v) for v in np.cumsum((0,) + STRIPS))
EDGES = EDGE_AT[-1]
f32, bf16 = jnp.float32, jnp.bfloat16
VMEM = pl.BlockSpec(memory_space=pltpu.VMEM)
PARAMS = pltpu.CompilerParams(vmem_limit_bytes=56 * 1024 * 1024)


def window():
    offsets = np.arange(11).astype(np.float32) - np.float32(5.0)
    shaped = np.exp(-offsets * offsets / np.float32(4.5))
    return (shaped / shaped.sum(dtype=np.float32)).astype(np.float32)


TAPS = [float(v) for v in window()]


def split(value):
    high = value.astype(bf16)
    return high, (value - high.astype(f32)).astype(bf16)


def column_band():
    row = lax.broadcasted_iota(jnp.int32, (256, 128), 0)
    col = lax.broadcasted_iota(jnp.int32, (256, 128), 1)
    band = jnp.zeros((256, 128), f32)
    for tap in range(11):
        band = jnp.where(row - col == 59 + tap, TAPS[tap], band)
    return band


def pair_matrix():
    row = lax.broadcasted_iota(jnp.int32, (256, 128), 0)
    col = lax.broadcasted_iota(jnp.int32, (256, 128), 1)
    lane = jnp.where(row >= 128, row - 128, row)
    half = lane // 2
    side = jnp.where(lane >= 64, half - 32, half + 96)
    goal = jnp.where(row < 128, half + 32, side)
    return jnp.where(goal == col, 0.25, 0.0).astype(bf16)


def lanes(rows):
    return lax.broadcasted_iota(jnp.int32, (rows, 128), 1)


def pyramid(levels, low_ref, high_ref, pair_ref):
    pair_ref[...] = pair_matrix()
    for k in range(1, 5):
        src, dst = levels[k - 1], levels[k]
        rows = POOLED[k]
        pairs = pair_ref[...]
        lower = lanes(rows) < 64

        def rowsum(u):
            return src[u, pl.ds(0, rows, stride=2), :] + src[u, pl.ds(1, rows, stride=2), :]

        count = STRIPS[k - 1]
        for s in range(STRIPS[k]):
            zero = jnp.zeros((rows, 128), f32)
            middle = rowsum(2 * s) if 2 * s < count else zero
            left = rowsum(2 * s - 1) if 0 <= 2 * s - 1 < count else zero
            right = rowsum(2 * s + 1) if 2 * s + 1 < count else zero
            both = jnp.concatenate([middle, jnp.where(lower, right, left)], axis=1)
            first = both.astype(bf16)
            rest = both - first.astype(f32)
            second, third = split(rest)
            total = jnp.dot(third, pairs, preferred_element_type=f32)
            total += jnp.dot(second, pairs, preferred_element_type=f32)
            total += jnp.dot(first, pairs, preferred_element_type=f32)
            dst[s, 0:rows] = total
    for k in range(5):
        at, n, rows = EDGE_AT[k], STRIPS[k], ROWS[k]
        high_ref[at : at + n] = levels[k][:, 0:8, :]
        if rows >= 8:
            low_ref[at : at + n] = levels[k][:, rows - 8 : rows, :]
        else:
            low_ref[at : at + n, 0 : 8 - rows] = jnp.zeros((n, 8 - rows, 128), f32)
            low_ref[at : at + n, 8 - rows : 8] = levels[k][:, 0:rows, :]


def sample_kernel(x_ref, *refs):
    levels, low_ref, high_ref, pair_ref = refs[0:5], refs[5], refs[6], refs[7]
    lower = lanes(80) < 64
    before = jnp.zeros((80, 128), f32)
    for s in range(STRIPS[0]):
        now = jnp.zeros((80, 128), f32)
        if s < TILES[0]:
            now = pltpu.roll(x_ref[0, :, 128 * s : 128 * s + 128], 64, 1)
        levels[0][s] = jnp.where(lower, before, now)
        before = now
    pyramid(levels, low_ref, high_ref, pair_ref)


def pack_kernel(t_ref, out_ref):
    out_ref[0:80] = t_ref[:, 0:128]
    parts = [t_ref[8 * a : 8 * a + 8, 128:140] for a in range(10)]
    out_ref[80:88] = jnp.concatenate(parts + [jnp.zeros((8, 8), f32)], axis=1)


def truth_kernel(g_ref, *refs):
    levels, low_ref, high_ref, pair_ref = refs[0:5], refs[5], refs[6], refs[7]
    me = lax.axis_index("samp")
    my_z, my_y = me // 4, me % 4
    held = {}
    lane = lanes(80)
    for s in range(32):
        dz = lax.rem(my_z - s // 4 + 8, 8)
        dy = lax.rem(my_y - s % 4 + 4, 4)
        at = pl.multiple_of((dz * 4 + dy) * 88, 8)
        start = 64 + 140 * s
        q, off = start // 128, start % 128
        main = pltpu.roll(g_ref[pl.ds(at, 80), :], off, 1)
        tail8 = g_ref[pl.ds(pl.multiple_of(at + 80, 8), 8), :]
        tail = jnp.concatenate([pltpu.roll(tail8, (off - 12 * a) % 128, 1) for a in range(10)], axis=0)
        held.setdefault(q, []).append((main, off, 128))
        held.setdefault(q + 1, []).append((main, 0, off))
        held.setdefault(q + 1, []).append((tail, off, min(128, off + 12)))
        if off + 12 > 128:
            held.setdefault(q + 2, []).append((tail, 0, off + 12 - 128))
        last = 35 if s == 31 else (64 + 140 * (s + 1)) // 128 - 1
        for tile in sorted(held):
            if tile <= last:
                value = jnp.zeros((80, 128), f32)
                for piece, lo, hi in held.pop(tile):
                    if hi > lo:
                        value = jnp.where((lane >= lo) & (lane < hi), piece, value)
                levels[0][tile] = value
    pyramid(levels, low_ref, high_ref, pair_ref)


def maps_kernel(*refs):
    xs, ts = refs[0:5], refs[5:10]
    x_low, x_high, t_low, t_high = refs[10:14]
    outs = refs[14:19]
    band_ref, fine_ref, fields, v_high, v_low, v_full = refs[19:25]
    fine_ref[...] = column_band()
    high, low = split(fine_ref[...])
    band_ref[:, 0:128] = high
    band_ref[:, 128:256] = low
    for k in range(5):
        rows, held, work, at = ROWS[k], HELD[k], WORK[k], EDGE_AT[k]
        span = work + 16

        def vertical(s, slot):
            for field, (ref, low, high) in enumerate(((xs[k], x_low, x_high), (ts[k], t_low, t_high))):
                fields[field, 0:8] = low[at + s]
                fields[field, 8 : 8 + held] = ref[s]
                fields[field, 8 + rows : 16 + rows] = high[at + s]
            x, t = fields[0, 0:span], fields[1, 0:span]
            fields[2, 0:span] = x * x
            fields[3, 0:span] = t * t
            fields[4, 0:span] = x * t
            for field in range(5):
                total = TAPS[5] * fields[field, 8 : 8 + work]
                for tap in range(5):
                    pair = fields[field, 3 + tap : 3 + tap + work] + fields[field, 13 - tap : 13 - tap + work]
                    total = total + TAPS[tap] * pair
                if k >= 2:
                    v_full[slot, field * work : (field + 1) * work] = total
                    continue
                high, low = split(total)
                v_high[slot, field * work : (field + 1) * work] = high
                v_low[slot, field * work : (field + 1) * work] = low

        def finish(first, second, width):
            n = 5 * work
            if k >= 2:
                both = jnp.concatenate([v_full[first, 0:n], v_full[second, 0:n]], axis=1)
                acc = jnp.dot(
                    both, fine_ref[...], precision=lax.Precision.HIGHEST, preferred_element_type=f32
                )
                return ratio(acc)[:, 0:width]
            band = band_ref[...]
            both = jnp.concatenate([v_high[first, 0:n], v_high[second, 0:n]], axis=1)
            acc = jnp.dot(both, band, preferred_element_type=f32)
            both = jnp.concatenate([v_low[first, 0:n], v_low[second, 0:n]], axis=1)
            acc += jnp.dot(both, band, preferred_element_type=f32)
            return ratio(acc[:, 0:128] + acc[:, 128:256])[:, 0:width]

        def ratio(acc):
            mean_x, mean_y, second_x, second_y, cross = (
                acc[f * work : f * work + rows] for f in range(5)
            )
            square_x, square_y, product = mean_x * mean_x, mean_y * mean_y, mean_x * mean_y
            covar = cross - product
            result = (2.0 * covar + small_two) / (
                (second_x - square_x) + (second_y - square_y) + small_two
            )
            if k == 4:
                result = (2.0 * product + small_one) / (square_x + square_y + small_one) * result
            return result

        out, tiles = outs[k], TILES[k]
        whole = COLS[k] // 128
        vertical(0, 0)

        @pl.loop(0, whole)
        def _(j):
            odd = lax.rem(j, 2)
            vertical(j + 1, 1 - odd)
            out[0, :, pl.ds(pl.multiple_of(j * 128, 128), 128)] = finish(odd, 1 - odd, 128)

        if whole < tiles:
            odd = whole % 2
            vertical(tiles, 1 - odd)
            width = COLS[k] - 128 * whole
            out[0, :, 128 * whole :] = finish(odd, 1 - odd, width)


def level_shapes():
    return [jax.ShapeDtypeStruct((STRIPS[k], HELD[k], 128), f32) for k in range(5)] + [
        jax.ShapeDtypeStruct((EDGES, 8, 128), f32)
    ] * 2


def shifted(n, stride, k):
    perm = []
    for i in range(32):
        c = (i // stride) % n
        perm.append((i, i + ((c + k) % n - c) * stride))
    return perm


def along_z(x, k):
    return lax.ppermute(x, "samp", shifted(8, 4, k))


def along_y(x, k):
    return lax.ppermute(x, "samp", shifted(4, 1, k))


def gather(x):
    group = jnp.concatenate([x, along_y(x, 1), along_y(x, 2), along_y(x, -1)], axis=0)
    up, down = [group], [group]
    for _ in range(4):
        up.append(along_z(up[-1], 1))
    for _ in range(3):
        down.append(along_z(down[-1], -1))
    return jnp.concatenate(up + [down[3], down[2], down[1]], axis=0)


def local(samples, truth_field):
    forward = [(i, i + 1) for i in range(7)]
    backward = [(i + 1, i) for i in range(7)]
    scratch = [pltpu.VMEM((256, 128), bf16)]
    prepare = functools.partial(
        pl.pallas_call,
        out_shape=level_shapes(),
        in_specs=[VMEM],
        out_specs=[VMEM] * 7,
        scratch_shapes=scratch,
        compiler_params=PARAMS,
    )
    packed = pl.pallas_call(
        pack_kernel,
        out_shape=jax.ShapeDtypeStruct((88, 128), f32),
        in_specs=[VMEM],
        out_specs=VMEM,
        name="pack",
    )(truth_field)
    whole = gather(packed)
    cost = pl.CostEstimate(flops=10**9, bytes_accessed=10**7, transcendentals=0)
    *xs, x_low, x_high = prepare(sample_kernel, name="samples", cost_estimate=cost)(samples)
    x_low = lax.ppermute(x_low, "rows", forward)
    x_high = lax.ppermute(x_high, "rows", backward)
    *ts, t_low, t_high = prepare(truth_kernel, name="truth", cost_estimate=cost)(whole)
    t_low = lax.ppermute(t_low, "rows", forward)
    t_high = lax.ppermute(t_high, "rows", backward)
    return tuple(
        pl.pallas_call(
            maps_kernel,
            out_shape=[jax.ShapeDtypeStruct((1, ROWS[k], COLS[k]), f32) for k in range(5)],
            in_specs=[VMEM] * 14,
            out_specs=[VMEM] * 5,
            scratch_shapes=[
                pltpu.VMEM((256, 256), bf16),
                pltpu.VMEM((256, 128), f32),
                pltpu.VMEM((5, 96, 128), f32),
                pltpu.VMEM((2, 400, 128), bf16),
                pltpu.VMEM((2, 400, 128), bf16),
                pltpu.VMEM((2, 160, 128), f32),
            ],
            compiler_params=PARAMS,
            name="maps",
        )(*xs, *ts, x_low, x_high, t_low, t_high)
    )


def solution(mesh):
    placed = (P("samp", "rows", None), P("rows", "samp"))
    return jax.shard_map(
        local,
        mesh=mesh,
        in_specs=placed,
        out_specs=(P("samp", "rows", None),) * 5,
        check_vma=False,
    )
```

```python
import functools

import jax
import jax.numpy as jnp
import numpy as np
from jax import lax
from jax.experimental import pallas as pl
from jax.experimental.pallas import tpu as pltpu
from jax.sharding import PartitionSpec as P

small_one = 0.0001
small_two = 0.0009

ROWS = (80, 40, 20, 10, 5)
COLS = (4480, 2240, 1120, 560, 280)
TILES = tuple(-(-c // 128) for c in COLS)
STRIPS = tuple(t + 1 for t in TILES)
HELD = (80, 48, 32, 16, 8)
POOLED = (80, 40, 24, 16, 8)
WORK = (80, 48, 32, 16, 16)
EDGE_AT = tuple(int(v) for v in np.cumsum((0,) + STRIPS))
EDGES = EDGE_AT[-1]
ORDER = (0, 1, 7, 3, 4, 2, 5, 6)
CHUNK = 9
f32, bf16 = jnp.float32, jnp.bfloat16
VMEM = pl.BlockSpec(memory_space=pltpu.VMEM)
ANYWHERE = pl.BlockSpec(memory_space=pl.ANY)
PARAMS = pltpu.CompilerParams(vmem_limit_bytes=20 * 1024 * 1024)


def window():
    offsets = np.arange(11).astype(np.float32) - np.float32(5.0)
    shaped = np.exp(-offsets * offsets / np.float32(4.5))
    return (shaped / shaped.sum(dtype=np.float32)).astype(np.float32)


TAPS = [float(v) for v in window()]


def split(value):
    high = value.astype(bf16)
    return high, (value - high.astype(f32)).astype(bf16)


def column_band():
    row = lax.broadcasted_iota(jnp.int32, (256, 128), 0)
    col = lax.broadcasted_iota(jnp.int32, (256, 128), 1)
    band = jnp.zeros((256, 128), f32)
    for tap in range(11):
        band = jnp.where(row - col == 59 + tap, TAPS[tap], band)
    return band


def pair_matrix():
    row = lax.broadcasted_iota(jnp.int32, (256, 128), 0)
    col = lax.broadcasted_iota(jnp.int32, (256, 128), 1)
    lane = jnp.where(row >= 128, row - 128, row)
    half = lane // 2
    side = jnp.where(lane >= 64, half - 32, half + 96)
    goal = jnp.where(row < 128, half + 32, side)
    return jnp.where(goal == col, 0.25, 0.0).astype(bf16)


def lanes(rows):
    return lax.broadcasted_iota(jnp.int32, (rows, 128), 1)


def pyramid(levels, low_ref, high_ref, pair_ref):
    pair_ref[...] = pair_matrix()
    for k in range(1, 5):
        src, dst = levels[k - 1], levels[k]
        rows = POOLED[k]
        pairs = pair_ref[...]
        lower = lanes(rows) < 64

        def rowsum(u):
            return src[u, pl.ds(0, rows, stride=2), :] + src[u, pl.ds(1, rows, stride=2), :]

        count = STRIPS[k - 1]
        for s in range(STRIPS[k]):
            zero = jnp.zeros((rows, 128), f32)
            middle = rowsum(2 * s) if 2 * s < count else zero
            left = rowsum(2 * s - 1) if 0 <= 2 * s - 1 < count else zero
            right = rowsum(2 * s + 1) if 2 * s + 1 < count else zero
            both = jnp.concatenate([middle, jnp.where(lower, right, left)], axis=1)
            first = both.astype(bf16)
            rest = both - first.astype(f32)
            second, third = split(rest)
            total = jnp.dot(third, pairs, preferred_element_type=f32)
            total += jnp.dot(second, pairs, preferred_element_type=f32)
            total += jnp.dot(first, pairs, preferred_element_type=f32)
            dst[s, 0:rows] = total
    for k in range(5):
        at, n, rows = EDGE_AT[k], STRIPS[k], ROWS[k]
        high_ref[at : at + n] = levels[k][:, 0:8, :]
        if rows >= 8:
            low_ref[at : at + n] = levels[k][:, rows - 8 : rows, :]
        else:
            low_ref[at : at + n, 0 : 8 - rows] = jnp.zeros((n, 8 - rows, 128), f32)
            low_ref[at : at + n, 8 - rows : 8] = levels[k][:, 0:rows, :]


def sample_kernel(x_ref, *refs):
    levels, low_ref, high_ref, pair_ref = refs[0:5], refs[5], refs[6], refs[7]
    lower = lanes(80) < 64
    before = jnp.zeros((80, 128), f32)
    for s in range(STRIPS[0]):
        now = jnp.zeros((80, 128), f32)
        if s < TILES[0]:
            now = pltpu.roll(x_ref[0, :, 128 * s : 128 * s + 128], 64, 1)
        levels[0][s] = jnp.where(lower, before, now)
        before = now
    pyramid(levels, low_ref, high_ref, pair_ref)


def pack_kernel(t_ref, out_ref):
    out_ref[0:80] = t_ref[0:128, :].T
    rest = t_ref[128:140, :].T
    parts = [rest[8 * a : 8 * a + 8] for a in range(10)]
    out_ref[80:88] = jnp.concatenate(parts + [jnp.zeros((8, 8), f32)], axis=1)


def truth_kernel(g_ref, *refs):
    refs = refs[2:]
    levels, low_ref, high_ref, pair_ref = refs[0:5], refs[5], refs[6], refs[7]
    me = lax.axis_index("samp")
    my_z, my_y = me // 4, me % 4
    held = {}
    lane = lanes(80)
    for s in range(32):
        dz = lax.rem(my_z - s // 4 + 8, 8)
        slot = dz
        for apart in (2, 5, 6, 7):
            slot = jnp.where(dz == apart, ORDER.index(apart), slot)
        dy = lax.rem(my_y - s % 4 + 4, 4)
        at = pl.multiple_of((dy * 8 + slot) * 88, 8)
        start = 64 + 140 * s
        q, off = start // 128, start % 128
        main = pltpu.roll(g_ref[pl.ds(at, 80), :], off, 1)
        tail8 = g_ref[pl.ds(pl.multiple_of(at + 80, 8), 8), :]
        tail = jnp.concatenate([pltpu.roll(tail8, (off - 12 * a) % 128, 1) for a in range(10)], axis=0)
        held.setdefault(q, []).append((main, off, 128))
        held.setdefault(q + 1, []).append((main, 0, off))
        held.setdefault(q + 1, []).append((tail, off, min(128, off + 12)))
        if off + 12 > 128:
            held.setdefault(q + 2, []).append((tail, 0, off + 12 - 128))
        last = 35 if s == 31 else (64 + 140 * (s + 1)) // 128 - 1
        for tile in sorted(held):
            if tile <= last:
                value = jnp.zeros((80, 128), f32)
                for piece, lo, hi in held.pop(tile):
                    if hi > lo:
                        value = jnp.where((lane >= lo) & (lane < hi), piece, value)
                levels[0][tile] = value
    pyramid(levels, low_ref, high_ref, pair_ref)


def set_bands(band_ref, fine_ref=None):
    band = column_band()
    high, low = split(band)
    band_ref[:, 0:128] = high
    band_ref[:, 128:256] = low
    if fine_ref is not None:
        fine_ref[...] = band


def row_sum(read, work):
    total = TAPS[5] * read(5, work)
    for tap in range(5):
        total = total + TAPS[tap] * (read(tap, work) + read(10 - tap, work))
    return total


def keep(at, slot, v_high, v_low, total):
    high, low = split(total)
    n = total.shape[0]
    v_high[slot, at : at + n] = high
    v_low[slot, at : at + n] = low


def column_sum(first, second, n, v_high, v_low, band_ref):
    band = band_ref[...]
    both = jnp.concatenate([v_high[first, 0:n], v_high[second, 0:n]], axis=1)
    acc = jnp.dot(both, band, preferred_element_type=f32)
    both = jnp.concatenate([v_low[first, 0:n], v_low[second, 0:n]], axis=1)
    acc += jnp.dot(both, band, preferred_element_type=f32)
    return acc[:, 0:128] + acc[:, 128:256]


def fine_sum(first, second, n, v_full, fine_ref):
    both = jnp.concatenate([v_full[first, 0:n], v_full[second, 0:n]], axis=1)
    return jnp.dot(
        both, fine_ref[...], precision=lax.Precision.HIGHEST, preferred_element_type=f32
    )


def ratio(mean_x, var_x, mean_y, second_y, cross, coarsest=False):
    square_y, product = mean_y * mean_y, mean_x * mean_y
    result = (2.0 * (cross - product) + small_two) / (
        var_x + (second_y - square_y) + small_two
    )
    if coarsest:
        result = (2.0 * product + small_one) / (mean_x * mean_x + square_y + small_one) * result
    return result


def fine_x_kernel(x_ref, x_next, low_ref, low_next, high_ref, high_next, mean_ref, var_ref, *scratch):
    band_ref, fields, v_high, v_low = scratch

    def vertical(x, low, high, slot):
        at = 2 * (slot % 3)
        fields[at, 0:8] = low
        fields[at, 8:88] = x
        fields[at, 88:96] = high
        whole = fields[at]
        fields[at + 1] = whole * whole
        for f in range(2):
            keep(80 * f, slot, v_high, v_low, row_sum(lambda i, n: fields[at + f, 3 + i : 3 + i + n], 80))

    def finish(j):
        acc = column_sum(j, j + 1, 160, v_high, v_low, band_ref)
        mean = acc[0:80]
        mean_ref[j] = mean
        var_ref[j] = acc[80:160] - mean * mean

    @pl.when(pl.program_id(0) == 0)
    def _():
        set_bands(band_ref)
        vertical(x_ref[0], low_ref[0], high_ref[0], 0)

    @pl.when(pl.program_id(0) > 0)
    def _():
        v_high[0] = v_high[CHUNK]
        v_low[0] = v_low[CHUNK]

    for j in range(CHUNK - 1):
        vertical(x_ref[j + 1], low_ref[j + 1], high_ref[j + 1], j + 1)
        finish(j)
    vertical(x_next[0], low_next[0], high_next[0], CHUNK)
    finish(CHUNK - 1)


def fine_t_kernel(x_ref, x_next, t_ref, t_next, mean_ref, var_ref, out_ref, *scratch):
    band_ref, fields, v_high, v_low = scratch

    def vertical(x, t, slot):
        at = 2 * (slot % 3)
        tv = t[...]
        fields[at] = tv * tv
        fields[at + 1] = x[...] * tv
        keep(0, slot, v_high, v_low, row_sum(lambda i, n: t[3 + i : 3 + i + n], 64))
        for f in range(2):
            total = row_sum(lambda i, n: fields[at + f, 3 + i : 3 + i + n], 64)
            keep(64 * f + 64, slot, v_high, v_low, total)

    def finish(j):
        acc = column_sum(j, j + 1, 192, v_high, v_low, band_ref)
        out_ref[0, 8:72, j * 128 : j * 128 + 128] = ratio(
            mean_ref[j, 8:72], var_ref[j, 8:72], acc[0:64], acc[64:128], acc[128:192]
        )

    @pl.when(pl.program_id(0) == 0)
    def _():
        set_bands(band_ref)
        vertical(x_ref.at[0], t_ref.at[0], 0)

    @pl.when(pl.program_id(0) > 0)
    def _():
        v_high[0] = v_high[CHUNK]
        v_low[0] = v_low[CHUNK]

    for j in range(CHUNK - 1):
        vertical(x_ref.at[j + 1], t_ref.at[j + 1], j + 1)
        finish(j)
    vertical(x_next.at[0], t_next.at[0], CHUNK)
    finish(CHUNK - 1)


def fill(fields, field, ref, low, high, k, s):
    at = EDGE_AT[k] + s
    fields[field, 0:8] = low[at]
    fields[field, 8 : 8 + HELD[k]] = ref[s]
    fields[field, 8 + ROWS[k] : 16 + ROWS[k]] = high[at]


def coarse_x_kernel(*refs):
    xs, (low, high), means, variances = refs[0:4], refs[4:6], refs[6:10], refs[10:14]
    band_ref, fine_ref, fields, v_high, v_low, v_full = refs[14:20]
    set_bands(band_ref, fine_ref)
    for k in range(1, 5):
        rows, work = ROWS[k], WORK[k]
        span = work + 16

        def vertical(s, slot):
            at = 2 * slot
            fill(fields, at, xs[k - 1], low, high, k, s)
            x = fields[at, 0:span]
            fields[at + 1, 0:span] = x * x
            for f in range(2):
                total = row_sum(lambda i, n: fields[at + f, 3 + i : 3 + i + n], work)
                if k >= 2:
                    v_full[slot, f * work : (f + 1) * work] = total
                else:
                    keep(f * work, slot, v_high, v_low, total)

        def finish(j, slot):
            if k >= 2:
                acc = fine_sum(slot, (slot + 1) % 3, 2 * work, v_full, fine_ref)
            else:
                acc = column_sum(slot, (slot + 1) % 3, 2 * work, v_high, v_low, band_ref)
            mean = acc[0:work]
            means[k - 1][j] = mean
            variances[k - 1][j] = acc[work : 2 * work] - mean * mean

        vertical(0, 0)

        for j in range(TILES[k]):
            vertical(j + 1, (j + 1) % 3)
            finish(j, j % 3)


def coarse_t_kernel(*refs):
    xs, ts = refs[0:4], refs[4:8]
    x_low, x_high, t_low, t_high = refs[8:12]
    means, variances = refs[12:16], refs[16:20]
    x_ends, t_ends, mean_ends, var_ends = refs[20:22], refs[22:24], refs[24:26], refs[26:28]
    out_fine, outs = refs[29], refs[30:34]
    band_ref, fine_ref, fields, v_high, v_low, v_full, ends, sems = refs[34:42]
    set_bands(band_ref, fine_ref)

    def rows_of(f, start):
        return lambda i, n: fields[f, start + 3 + i : start + 3 + i + n]

    def vertical(s, slot):
        for f, (two, low, high) in enumerate(((t_ends, t_low, t_high), (x_ends, x_low, x_high))):
            fields[3 * slot + f, 0:8] = low[s]
            fields[3 * slot + f, 8:24] = two[0][s]
            fields[3 * slot + f, 24:40] = two[1][s]
            fields[3 * slot + f, 40:48] = high[s]
        t, x = fields[3 * slot, 0:48], fields[3 * slot + 1, 0:48]
        fields[3 * slot + 1, 0:48] = t * t
        fields[3 * slot + 2, 0:48] = x * t
        for f in range(3):
            top = row_sum(rows_of(3 * slot + f, 0), 8)
            bottom = row_sum(rows_of(3 * slot + f, 24), 8)
            keep(16 * f, slot, v_high, v_low, jnp.concatenate([top, bottom], axis=0))

    def finish(j, slot):
        acc = column_sum(slot, (slot + 1) % 3, 48, v_high, v_low, band_ref)
        for end in range(2):
            at = 8 * end
            ends[end, :, j * 128 : j * 128 + 128] = ratio(
                mean_ends[end][j],
                var_ends[end][j],
                acc[at : at + 8],
                acc[16 + at : 24 + at],
                acc[32 + at : 40 + at],
            )

    vertical(0, 0)

    for j in range(TILES[0]):
        vertical(j + 1, (j + 1) % 3)
        finish(j, j % 3)

    copies = [
        pltpu.make_async_copy(ends.at[end], out_fine.at[0, pl.ds(72 * end, 8), :], sems.at[end])
        for end in range(2)
    ]
    for copy in copies:
        copy.start()

    for k in range(1, 5):
        rows, work = ROWS[k], WORK[k]
        span = work + 16

        def vertical(s, slot):
            at = 3 * slot
            fill(fields, at, ts[k - 1], t_low, t_high, k, s)
            fill(fields, at + 1, xs[k - 1], x_low, x_high, k, s)
            t, x = fields[at, 0:span], fields[at + 1, 0:span]
            fields[at + 1, 0:span] = t * t
            fields[at + 2, 0:span] = x * t
            for f in range(3):
                total = row_sum(rows_of(at + f, 0), work)
                if k >= 2:
                    v_full[slot, f * work : (f + 1) * work] = total
                else:
                    keep(f * work, slot, v_high, v_low, total)

        def finish(j, slot, width):
            if k >= 2:
                acc = fine_sum(slot, (slot + 1) % 3, 3 * work, v_full, fine_ref)
            else:
                acc = column_sum(slot, (slot + 1) % 3, 3 * work, v_high, v_low, band_ref)
            parts = (acc[f * work : f * work + rows] for f in range(3))
            value = ratio(means[k - 1][j, 0:rows], variances[k - 1][j, 0:rows], *parts, k == 4)
            return value[:, 0:width]

        out, tiles = outs[k - 1], TILES[k]
        whole = COLS[k] // 128
        vertical(0, 0)

        for j in range(tiles):
            vertical(j + 1, (j + 1) % 3)
            cols = pl.ds(128 * j, 128 if j < whole else COLS[k] - 128 * whole)
            if k == 1:
                out[0, :, cols] = finish(j, j % 3, cols.size)
            else:
                out[:, 0, cols] = finish(j, j % 3, cols.size)

    for copy in copies:
        copy.wait()


def level_shapes():
    return [jax.ShapeDtypeStruct((STRIPS[k], HELD[k], 128), f32) for k in range(5)] + [
        jax.ShapeDtypeStruct((EDGES, 8, 128), f32)
    ] * 2


def shifted(n, stride, k):
    perm = []
    for i in range(32):
        c = (i // stride) % n
        perm.append((i, i + ((c + k) % n - c) * stride))
    return perm


def along_z(x, k):
    return lax.ppermute(x, "samp", shifted(8, 4, k))


def along_y(x, k):
    return lax.ppermute(x, "samp", shifted(4, 1, k))


def join_kernel(*refs):
    out_ref = refs[-1]
    at = 0
    for ref in refs[:-2]:
        n = ref.shape[0]
        out_ref[at : at + n] = ref[...]
        at += n


def join(parts, before):
    rows = sum(part.shape[0] for part in parts)
    return pl.pallas_call(
        join_kernel,
        out_shape=jax.ShapeDtypeStruct((rows, 128), f32),
        in_specs=[VMEM] * len(parts) + [ANYWHERE],
        out_specs=VMEM,
        compiler_params=PARAMS,
        cost_estimate=cost(0.02),
        name="join",
    )(*parts, before)


def cut(column, half, before):
    n = column.shape[0] // 2
    return pl.pallas_call(
        lambda ref, _, out_ref: join_kernel(ref, _, out_ref),
        grid=(1,),
        out_shape=jax.ShapeDtypeStruct((n, 128), f32),
        in_specs=[pl.BlockSpec((n, 128), lambda g: (half, 0)), ANYWHERE],
        out_specs=VMEM,
        compiler_params=PARAMS,
        cost_estimate=cost(0.02),
        name="cut",
    )(column, before)


def chunk_spec(rows, base, step=None):
    if step is None:
        return pl.BlockSpec((CHUNK, rows, 128), lambda g: (g + base, 0, 0))
    return pl.BlockSpec(
        (1, rows, 128), lambda g: (jnp.minimum((g + base + 1) * CHUNK, STRIPS[0] - 1), 0, 0)
    )


def both_specs(rows, base):
    return [chunk_spec(rows, base), chunk_spec(rows, base, 1)]


def cost(micros):
    return pl.CostEstimate(flops=0, bytes_accessed=int(micros * 5e7), transcendentals=0)


def fine_x(x, low, high, *before):
    return pl.pallas_call(
        lambda *refs: fine_x_kernel(*refs[0:6], *refs[6 + len(before) :]),
        grid=(STRIPS[0] // CHUNK,),
        out_shape=[jax.ShapeDtypeStruct((STRIPS[0], 80, 128), f32)] * 2,
        in_specs=both_specs(80, 0) + both_specs(8, 0) + both_specs(8, 0) + [ANYWHERE] * len(before),
        out_specs=[chunk_spec(80, 0)] * 2,
        scratch_shapes=[
            pltpu.VMEM((256, 256), bf16),
            pltpu.VMEM((6, 96, 128), f32),
            pltpu.VMEM((CHUNK + 1, 160, 128), bf16),
            pltpu.VMEM((CHUNK + 1, 160, 128), bf16),
        ],
        compiler_params=PARAMS,
        cost_estimate=cost(5),
        name="fine_x",
    )(x, x, low, low, high, high, *before)


def coarse_x(xs, low, high, *before):
    shapes = [jax.ShapeDtypeStruct((TILES[k], WORK[k], 128), f32) for k in range(1, 5)]
    return pl.pallas_call(
        lambda *refs: coarse_x_kernel(*refs[0:6], *refs[6 + len(before) :]),
        out_shape=shapes * 2,
        in_specs=[VMEM] * 6 + [ANYWHERE] * len(before),
        out_specs=[VMEM] * 8,
        scratch_shapes=[
            pltpu.VMEM((256, 256), bf16),
            pltpu.VMEM((256, 128), f32),
            pltpu.VMEM((6, 64, 128), f32),
            pltpu.VMEM((3, 96, 128), bf16),
            pltpu.VMEM((3, 96, 128), bf16),
            pltpu.VMEM((3, 64, 128), f32),
        ],
        compiler_params=PARAMS,
        cost_estimate=cost(5),
        name="coarse_x",
    )(*xs[1:], low, high, *before)


def fine_t(x, t, mean, var):
    return pl.pallas_call(
        fine_t_kernel,
        grid=(STRIPS[0] // CHUNK,),
        out_shape=jax.ShapeDtypeStruct((1, 80, COLS[0]), f32),
        in_specs=both_specs(80, 0) + both_specs(80, 0) + [chunk_spec(80, 0)] * 2,
        out_specs=pl.BlockSpec((1, 80, 128 * CHUNK), lambda g: (0, 0, g)),
        scratch_shapes=[
            pltpu.VMEM((256, 256), bf16),
            pltpu.VMEM((6, 80, 128), f32),
            pltpu.VMEM((CHUNK + 1, 192, 128), bf16),
            pltpu.VMEM((CHUNK + 1, 192, 128), bf16),
        ],
        compiler_params=PARAMS,
        cost_estimate=cost(8),
        name="fine_t",
    )(x, x, t, t, mean, var)


def coarse_t(xs, ts, edges, coarse, mean, var, fine):
    def ends(rows, last):
        return [
            pl.BlockSpec((STRIPS[0], rows, 128), lambda g: (0, 0, 0)),
            pl.BlockSpec((STRIPS[0], rows, 128), lambda g: (0, last, 0)),
        ]

    shapes = [jax.ShapeDtypeStruct((1, 80, COLS[0]), f32), jax.ShapeDtypeStruct((1, 40, COLS[1]), f32)]
    shapes += [jax.ShapeDtypeStruct((ROWS[k], 1, COLS[k]), f32) for k in range(2, 5)]
    fine, half, *rest = pl.pallas_call(
        coarse_t_kernel,
        grid=(1,),
        out_shape=shapes,
        in_specs=[VMEM] * 20 + ends(16, 4) * 2 + ends(8, 9) * 2 + [ANYWHERE],
        out_specs=[ANYWHERE] + [VMEM] * 4,
        input_output_aliases={28: 0},
        scratch_shapes=[
            pltpu.VMEM((256, 256), bf16),
            pltpu.VMEM((256, 128), f32),
            pltpu.VMEM((9, 64, 128), f32),
            pltpu.VMEM((3, 144, 128), bf16),
            pltpu.VMEM((3, 144, 128), bf16),
            pltpu.VMEM((3, 96, 128), f32),
            pltpu.VMEM((2, 8, COLS[0]), f32),
            pltpu.SemaphoreType.DMA((2,)),
        ],
        compiler_params=PARAMS,
        name="coarse_t",
    )(*xs[1:], *ts[1:], *edges, *coarse, xs[0], xs[0], ts[0], ts[0], mean, mean, var, var, fine)
    return (fine, half) + tuple(value.transpose(1, 0, 2) for value in rest)


def local(samples, truth_field):
    forward = [(i, i + 1) for i in range(7)]
    backward = [(i + 1, i) for i in range(7)]
    prepare = functools.partial(
        pl.pallas_call,
        out_shape=level_shapes(),
        in_specs=[VMEM],
        out_specs=[VMEM] * 7,
        scratch_shapes=[pltpu.VMEM((256, 128), bf16)],
        compiler_params=PARAMS,
        cost_estimate=cost(4),
    )
    packed = pl.pallas_call(
        pack_kernel,
        out_shape=jax.ShapeDtypeStruct((88, 128), f32),
        in_specs=[VMEM],
        out_specs=VMEM,
        name="pack",
    )(truth_field.T)
    three = jnp.concatenate([packed, along_z(packed, 1), along_z(packed, -1)], axis=0)
    far = [along_z(three, 3), along_z(three[0:176], -3)]
    *xs, x_low, x_high = prepare(
        lambda x_ref, _, *refs: sample_kernel(x_ref, *refs), name="samples", in_specs=[VMEM, ANYWHERE]
    )(samples, three)
    column = join([three, *far], x_low)
    x_low = lax.ppermute(x_low, "rows", forward)
    x_high = lax.ppermute(x_high, "rows", backward)
    up, down = along_y(column, 1), along_y(column, -1)
    mean, var = fine_x(xs[0], x_low, x_high, column)
    far = [along_y(cut(up, 0, mean), 1), along_y(cut(down, 1, mean), -1)]
    coarse = coarse_x(xs, x_low, x_high, up, down)
    whole = jnp.concatenate([column, up, *far, down], axis=0)
    *ts, t_low, t_high = prepare(truth_kernel, name="truth", in_specs=[VMEM, ANYWHERE, ANYWHERE])(
        whole, mean, coarse[3]
    )
    t_low = lax.ppermute(t_low, "rows", forward)
    t_high = lax.ppermute(t_high, "rows", backward)
    fine = fine_t(xs[0], ts[0], mean, var)
    return coarse_t(xs, ts, (x_low, x_high, t_low, t_high), coarse, mean, var, fine)


def solution(mesh):
    placed = (P("samp", "rows", None), P("rows", "samp"))
    return jax.shard_map(
        local,
        mesh=mesh,
        in_specs=placed,
        out_specs=(P("samp", "rows", None),) * 5,
        check_vma=False,
    )
```

```python
import functools

import jax
import jax.numpy as jnp
import numpy as np
from jax import lax
from jax.experimental import pallas as pl
from jax.experimental.pallas import tpu as pltpu
from jax.sharding import PartitionSpec as P

small_one = 0.0001
small_two = 0.0009

ROWS = (80, 40, 20, 10, 5)
COLS = (4480, 2240, 1120, 560, 280)
TILES = tuple(-(-c // 128) for c in COLS)
STRIPS = tuple(t + 1 for t in TILES)
HELD = (80, 48, 32, 16, 8)
POOLED = (80, 40, 24, 16, 8)
WORK = (80, 48, 32, 16, 16)
EDGE_AT = tuple(int(v) for v in np.cumsum((0,) + STRIPS))
EDGES = EDGE_AT[-1]
ORDER = (0, 1, 7, 3, 4, 2, 5, 6)
GROUP = 9
CHUNK = 9
f32, bf16 = jnp.float32, jnp.bfloat16
VMEM = pl.BlockSpec(memory_space=pltpu.VMEM)
ANYWHERE = pl.BlockSpec(memory_space=pl.ANY)
PARAMS = pltpu.CompilerParams(vmem_limit_bytes=20 * 1024 * 1024)


def window():
    offsets = np.arange(11).astype(np.float32) - np.float32(5.0)
    shaped = np.exp(-offsets * offsets / np.float32(4.5))
    return (shaped / shaped.sum(dtype=np.float32)).astype(np.float32)


TAPS = [float(v) for v in window()]


def split(value):
    high = value.astype(bf16)
    return high, (value - high.astype(f32)).astype(bf16)


def column_band():
    row = lax.broadcasted_iota(jnp.int32, (256, 128), 0)
    col = lax.broadcasted_iota(jnp.int32, (256, 128), 1)
    band = jnp.zeros((256, 128), f32)
    for tap in range(11):
        band = jnp.where(row - col == 59 + tap, TAPS[tap], band)
    return band


def pair_matrix():
    row = lax.broadcasted_iota(jnp.int32, (256, 128), 0)
    col = lax.broadcasted_iota(jnp.int32, (256, 128), 1)
    lane = jnp.where(row >= 128, row - 128, row)
    half = lane // 2
    side = jnp.where(lane >= 64, half - 32, half + 96)
    goal = jnp.where(row < 128, half + 32, side)
    return jnp.where(goal == col, 0.25, 0.0).astype(bf16)


def lanes(rows):
    return lax.broadcasted_iota(jnp.int32, (rows, 128), 1)


def pyramid(levels, low_ref, high_ref, pair_ref):
    pair_ref[...] = pair_matrix()
    for k in range(1, 5):
        src, dst = levels[k - 1], levels[k]
        rows = POOLED[k]
        pairs = pair_ref[...]
        lower = lanes(rows) < 64

        def rowsum(u):
            return src[u, pl.ds(0, rows, stride=2), :] + src[u, pl.ds(1, rows, stride=2), :]

        count = STRIPS[k - 1]
        for s in range(STRIPS[k]):
            zero = jnp.zeros((rows, 128), f32)
            middle = rowsum(2 * s) if 2 * s < count else zero
            left = rowsum(2 * s - 1) if 0 <= 2 * s - 1 < count else zero
            right = rowsum(2 * s + 1) if 2 * s + 1 < count else zero
            both = jnp.concatenate([middle, jnp.where(lower, right, left)], axis=1)
            first = both.astype(bf16)
            rest = both - first.astype(f32)
            second, third = split(rest)
            total = jnp.dot(third, pairs, preferred_element_type=f32)
            total += jnp.dot(second, pairs, preferred_element_type=f32)
            total += jnp.dot(first, pairs, preferred_element_type=f32)
            dst[s, 0:rows] = total
    for k in range(5):
        at, n, rows = EDGE_AT[k], STRIPS[k], ROWS[k]
        high_ref[at : at + n] = levels[k][:, 0:8, :]
        if rows >= 8:
            low_ref[at : at + n] = levels[k][:, rows - 8 : rows, :]
        else:
            low_ref[at : at + n, 0 : 8 - rows] = jnp.zeros((n, 8 - rows, 128), f32)
            low_ref[at : at + n, 8 - rows : 8] = levels[k][:, 0:rows, :]


def sample_kernel(x_ref, *refs):
    levels, low_ref, high_ref, pair_ref = refs[0:5], refs[5], refs[6], refs[7]
    lower = lanes(80) < 64
    before = jnp.zeros((80, 128), f32)
    for s in range(STRIPS[0]):
        now = jnp.zeros((80, 128), f32)
        if s < TILES[0]:
            now = pltpu.roll(x_ref[0, :, 128 * s : 128 * s + 128], 64, 1)
        levels[0][s] = jnp.where(lower, before, now)
        before = now
    pyramid(levels, low_ref, high_ref, pair_ref)


def pack_kernel(t_ref, out_ref):
    out_ref[0:80] = t_ref[0:128, :].T
    rest = t_ref[128:140, :].T
    parts = [rest[8 * a : 8 * a + 8] for a in range(10)]
    out_ref[80:88] = jnp.concatenate(parts + [jnp.zeros((8, 8), f32)], axis=1)


def truth_kernel(g_ref, *refs):
    refs = refs[1:]
    levels, low_ref, high_ref, pair_ref = refs[0:5], refs[5], refs[6], refs[7]
    me = lax.axis_index("samp")
    my_z, my_y = me // 4, me % 4
    held = {}
    lane = lanes(80)
    for s in range(32):
        dz = lax.rem(my_z - s // 4 + 8, 8)
        slot = dz
        for apart in (2, 5, 6, 7):
            slot = jnp.where(dz == apart, ORDER.index(apart), slot)
        dy = lax.rem(my_y - s % 4 + 4, 4)
        at = pl.multiple_of((dy * 8 + slot) * 88, 8)
        start = 64 + 140 * s
        q, off = start // 128, start % 128
        main = pltpu.roll(g_ref[pl.ds(at, 80), :], off, 1)
        tail8 = g_ref[pl.ds(pl.multiple_of(at + 80, 8), 8), :]
        tail = jnp.concatenate([pltpu.roll(tail8, (off - 12 * a) % 128, 1) for a in range(10)], axis=0)
        held.setdefault(q, []).append((main, off, 128))
        held.setdefault(q + 1, []).append((main, 0, off))
        held.setdefault(q + 1, []).append((tail, off, min(128, off + 12)))
        if off + 12 > 128:
            held.setdefault(q + 2, []).append((tail, 0, off + 12 - 128))
        last = 35 if s == 31 else (64 + 140 * (s + 1)) // 128 - 1
        for tile in sorted(held):
            if tile <= last:
                value = jnp.zeros((80, 128), f32)
                for piece, lo, hi in held.pop(tile):
                    if hi > lo:
                        value = jnp.where((lane >= lo) & (lane < hi), piece, value)
                levels[0][tile] = value
    pyramid(levels, low_ref, high_ref, pair_ref)


def set_bands(band_ref, third_ref=None):
    band = column_band()
    high, low = split(band)
    band_ref[:, 0:128] = high
    band_ref[:, 128:256] = low
    if third_ref is not None:
        third_ref[...] = ((band - high.astype(f32)) - low.astype(f32)).astype(bf16)


def row_sum(read, work):
    total = TAPS[5] * read(5, work)
    for tap in range(5):
        total = total + TAPS[tap] * (read(tap, work) + read(10 - tap, work))
    return total


def keep(at, slot, parts, total):
    n = total.shape[0]
    for p, ref in enumerate(parts):
        part = total.astype(bf16)
        ref[slot, at : at + n] = part
        if p + 1 < len(parts):
            total = total - part.astype(f32)


def column_sum(j, count, n, parts, band_ref, third_ref=None):
    def pairs(ref):
        return jnp.concatenate(
            [
                ref[j : j + count, 0:n].reshape(count * n, 128),
                ref[j + 1 : j + count + 1, 0:n].reshape(count * n, 128),
            ],
            axis=1,
        )

    acc = None
    for ref in reversed(parts):
        one = jnp.dot(pairs(ref), band_ref[...], preferred_element_type=f32)
        acc = one if acc is None else acc + one
    acc = acc[:, 0:128] + acc[:, 128:256]
    if third_ref is not None:
        acc = jnp.dot(pairs(parts[0]), third_ref[...], preferred_element_type=f32) + acc
    return acc


def ratio(mean_x, var_x, mean_y, second_y, cross, coarsest=False):
    square_y, product = mean_y * mean_y, mean_x * mean_y
    result = (2.0 * (cross - product) + small_two) / (
        var_x + (second_y - square_y) + small_two
    )
    if coarsest:
        result = (2.0 * product + small_one) / (mean_x * mean_x + square_y + small_one) * result
    return result


def fine_x_kernel(x_ref, x_next, mean_ref, var_ref, *scratch):
    band_ref, fields, v_high, v_low = scratch

    def vertical(x, slot):
        at = slot % 3
        value = x[...]
        fields[at] = value * value
        keep(0, slot, (v_high, v_low), row_sum(lambda i, n: x[3 + i : 3 + i + n], 64))
        total = row_sum(lambda i, n: fields[at, 3 + i : 3 + i + n], 64)
        keep(64, slot, (v_high, v_low), total)

    def finish(j):
        acc = column_sum(j, GROUP, 128, (v_high, v_low), band_ref)
        for g in range(GROUP):
            mean = acc[128 * g : 128 * g + 64]
            mean_ref[j + g] = mean
            var_ref[j + g] = acc[128 * g + 64 : 128 * g + 128] - mean * mean

    @pl.when(pl.program_id(0) == 0)
    def _():
        set_bands(band_ref)
        vertical(x_ref.at[0], 0)

    @pl.when(pl.program_id(0) > 0)
    def _():
        v_high[0] = v_high[CHUNK]
        v_low[0] = v_low[CHUNK]

    for j in range(CHUNK - 1):
        vertical(x_ref.at[j + 1], j + 1)
        if (j + 1) % GROUP == 0:
            finish(j + 1 - GROUP)
    vertical(x_next.at[0], CHUNK)
    finish(CHUNK - GROUP)


def fine_t_kernel(x_ref, x_next, t_ref, t_next, mean_ref, var_ref, out_ref, *scratch):
    band_ref, fields, v_high, v_low = scratch

    def vertical(x, t, slot):
        at = 2 * (slot % 3)
        tv = t[...]
        fields[at] = tv * tv
        fields[at + 1] = x[...] * tv
        keep(0, slot, (v_high, v_low), row_sum(lambda i, n: t[3 + i : 3 + i + n], 64))
        for f in range(2):
            total = row_sum(lambda i, n: fields[at + f, 3 + i : 3 + i + n], 64)
            keep(64 * f + 64, slot, (v_high, v_low), total)

    def finish(first):
        acc = column_sum(first, GROUP, 192, (v_high, v_low), band_ref)
        for g in range(GROUP):
            j, at = first + g, 192 * g
            out_ref[0, 8:72, j * 128 : j * 128 + 128] = ratio(
                mean_ref[j],
                var_ref[j],
                acc[at : at + 64],
                acc[at + 64 : at + 128],
                acc[at + 128 : at + 192],
            )

    @pl.when(pl.program_id(0) == 0)
    def _():
        set_bands(band_ref)
        vertical(x_ref.at[0], t_ref.at[0], 0)

    @pl.when(pl.program_id(0) > 0)
    def _():
        v_high[0] = v_high[CHUNK]
        v_low[0] = v_low[CHUNK]

    for j in range(CHUNK - 1):
        vertical(x_ref.at[j + 1], t_ref.at[j + 1], j + 1)
        if (j + 1) % GROUP == 0:
            finish(j + 1 - GROUP)
    vertical(x_next.at[0], t_next.at[0], CHUNK)
    finish(CHUNK - GROUP)


def groups(count, most):
    return [(first, min(most, count - first)) for first in range(0, count, most)]


def rest_x_kernel(*refs):
    xs, (low, high), x_ends = refs[0:4], refs[4:6], refs[6:8]
    means, variances = refs[8:13], refs[13:18]
    band_ref, third_ref, fields = refs[18:21]
    v_parts = refs[21:24]
    set_bands(band_ref, third_ref)

    def rows_of(f, start):
        return lambda i, n: fields[f, start + 3 + i : start + 3 + i + n]

    def store(k, first, count, work, acc):
        for g in range(count):
            row = 2 * work * g
            mean = acc[row : row + work]
            means[k][first + g] = mean
            variances[k][first + g] = acc[row + work : row + 2 * work] - mean * mean

    for s in range(STRIPS[0]):
        at = 2 * (s % 3)
        fields[at, 0:8] = low[s]
        fields[at, 8:24] = x_ends[0][s]
        fields[at, 24:40] = x_ends[1][s]
        fields[at, 40:48] = high[s]
        x = fields[at, 0:48]
        fields[at + 1, 0:48] = x * x
        for f in range(2):
            top = row_sum(rows_of(at + f, 0), 8)
            bottom = row_sum(rows_of(at + f, 24), 8)
            keep(16 * f, s, v_parts[0:2], jnp.concatenate([top, bottom], axis=0))
    for first, count in groups(TILES[0], 9):
        store(0, first, count, 16, column_sum(first, count, 32, v_parts[0:2], band_ref))
    for k in range(1, 5):
        rows, work, held = ROWS[k], WORK[k], HELD[k]
        parts, third = (v_parts, third_ref) if k >= 2 else (v_parts[0:2], None)
        for s in range(STRIPS[k]):
            at, edge = 2 * (s % 3), EDGE_AT[k] + s
            fields[at, 0:8] = low[edge]
            fields[at, 8 : 8 + held] = xs[k - 1][s]
            fields[at, 8 + rows : 16 + rows] = high[edge]
            x = fields[at, 0 : work + 16]
            fields[at + 1, 0 : work + 16] = x * x
            for f in range(2):
                keep(f * work, s, parts, row_sum(rows_of(at + f, 0), work))
        for first, count in groups(TILES[k], 9):
            acc = column_sum(first, count, 2 * work, parts, band_ref, third)
            store(k, first, count, work, acc)


def rest_kernel(*refs):
    xs, ts = refs[0:4], refs[4:8]
    x_low, x_high, t_low, t_high = refs[8:12]
    means, variances = refs[12:17], refs[17:22]
    x_ends, t_ends = refs[22:24], refs[24:26]
    out_fine, outs = refs[27], refs[28:32]
    band_ref, third_ref, fields = refs[32:35]
    v_parts, ends, sems = refs[35:38], refs[38], refs[39]
    set_bands(band_ref, third_ref)

    def rows_of(f, start):
        return lambda i, n: fields[f, start + 3 + i : start + 3 + i + n]

    def products(at, span):
        t, x = fields[at, 0:span], fields[at + 1, 0:span]
        fields[at + 1, 0:span] = t * t
        fields[at + 2, 0:span] = x * t

    for s in range(STRIPS[0]):
        at = 3 * (s % 3)
        for f, (two, low, high) in enumerate(((t_ends, t_low, t_high), (x_ends, x_low, x_high))):
            fields[at + f, 0:8] = low[s]
            fields[at + f, 8:24] = two[0][s]
            fields[at + f, 24:40] = two[1][s]
            fields[at + f, 40:48] = high[s]
        products(at, 48)
        for f in range(3):
            top = row_sum(rows_of(at + f, 0), 8)
            bottom = row_sum(rows_of(at + f, 24), 8)
            keep(16 * f, s, v_parts[0:2], jnp.concatenate([top, bottom], axis=0))
    for first, count in groups(TILES[0], 9):
        acc = column_sum(first, count, 48, v_parts[0:2], band_ref)
        for g in range(count):
            for end in range(2):
                j, row, side = first + g, 48 * g + 8 * end, slice(8 * end, 8 * end + 8)
                ends[end, :, 128 * j : 128 * j + 128] = ratio(
                    means[0][j, side],
                    variances[0][j, side],
                    acc[row : row + 8],
                    acc[row + 16 : row + 24],
                    acc[row + 32 : row + 40],
                )

    copies = [
        pltpu.make_async_copy(ends.at[end], out_fine.at[0, pl.ds(72 * end, 8), :], sems.at[end])
        for end in range(2)
    ]
    for copy in copies:
        copy.start()

    for k in range(1, 5):
        rows, work, held = ROWS[k], WORK[k], HELD[k]
        parts, third = (v_parts, third_ref) if k >= 2 else (v_parts[0:2], None)
        for s in range(STRIPS[k]):
            at, edge = 3 * (s % 3), EDGE_AT[k] + s
            for f, (ref, low, high) in enumerate(
                ((ts[k - 1], t_low, t_high), (xs[k - 1], x_low, x_high))
            ):
                fields[at + f, 0:8] = low[edge]
                fields[at + f, 8 : 8 + held] = ref[s]
                fields[at + f, 8 + rows : 16 + rows] = high[edge]
            products(at, work + 16)
            for f in range(3):
                keep(f * work, s, parts, row_sum(rows_of(at + f, 0), work))
        for first, count in groups(TILES[k], 9):
            acc = column_sum(first, count, 3 * work, parts, band_ref, third)
            for g in range(count):
                j, row, col = first + g, 3 * work * g, 128 * (first + g)
                three = (acc[row + f * work : row + f * work + rows] for f in range(3))
                map_ = ratio(means[k][j, 0:rows], variances[k][j, 0:rows], *three, k == 4)
                width = min(128, COLS[k] - col)
                if k == 1:
                    outs[0][0, :, col : col + width] = map_[:, 0:width]
                else:
                    outs[k - 1][:, 0, col : col + width] = map_[:, 0:width]

    for copy in copies:
        copy.wait()


def level_shapes():
    return [jax.ShapeDtypeStruct((STRIPS[k], HELD[k], 128), f32) for k in range(5)] + [
        jax.ShapeDtypeStruct((EDGES, 8, 128), f32)
    ] * 2


def shifted(n, stride, k):
    perm = []
    for i in range(32):
        c = (i // stride) % n
        perm.append((i, i + ((c + k) % n - c) * stride))
    return perm


def along_z(x, k):
    return lax.ppermute(x, "samp", shifted(8, 4, k))


def along_y(x, k):
    return lax.ppermute(x, "samp", shifted(4, 1, k))


def join_kernel(parts, outs):
    at = 0
    for part in parts:
        for out in outs:
            n = min(part.shape[0], out.shape[0] - at)
            if n > 0:
                out[at : at + n] = part[0:n]
        at += part.shape[0]


def join(parts, *before, head=None):
    rows, n = sum(part.shape[0] for part in parts), len(parts)
    sizes = [rows] if head is None else [rows, head]
    return pl.pallas_call(
        lambda *refs: join_kernel(refs[:n], refs[n + len(before) :]),
        out_shape=[jax.ShapeDtypeStruct((size, 128), f32) for size in sizes],
        in_specs=[VMEM] * n + [ANYWHERE] * len(before),
        out_specs=[VMEM] * len(sizes),
        compiler_params=PARAMS,
        cost_estimate=cost(0.02),
        name="join",
    )(*parts, *before)


def cut_kernel(up_ref, down_ref, first_ref, second_ref):
    n = first_ref.shape[0]
    first_ref[...] = up_ref[0:n]
    second_ref[...] = down_ref[n:]


def cut(up, down):
    n = up.shape[0] // 2
    return pl.pallas_call(
        cut_kernel,
        out_shape=[jax.ShapeDtypeStruct((n, 128), f32)] * 2,
        in_specs=[VMEM, VMEM],
        out_specs=[VMEM, VMEM],
        compiler_params=PARAMS,
        cost_estimate=cost(0.02),
        name="cut",
    )(up, down)


def chunk_spec(rows, base, step=None):
    if step is None:
        return pl.BlockSpec((CHUNK, rows, 128), lambda g: (g + base, 0, 0))
    return pl.BlockSpec(
        (1, rows, 128), lambda g: (jnp.minimum((g + base + 1) * CHUNK, STRIPS[0] - 1), 0, 0)
    )


def both_specs(rows, base):
    return [chunk_spec(rows, base), chunk_spec(rows, base, 1)]


def cost(micros):
    return pl.CostEstimate(flops=0, bytes_accessed=int(micros * 5e7), transcendentals=0)


def fine_x(x):
    return pl.pallas_call(
        fine_x_kernel,
        grid=(STRIPS[0] // CHUNK,),
        out_shape=[jax.ShapeDtypeStruct((STRIPS[0], 64, 128), f32)] * 2,
        in_specs=both_specs(80, 0),
        out_specs=[chunk_spec(64, 0)] * 2,
        scratch_shapes=[
            pltpu.VMEM((256, 256), bf16),
            pltpu.VMEM((3, 80, 128), f32),
            pltpu.VMEM((CHUNK + 1, 128, 128), bf16),
            pltpu.VMEM((CHUNK + 1, 128, 128), bf16),
        ],
        compiler_params=PARAMS,
        cost_estimate=cost(5),
        name="fine_x",
    )(x, x)


def fine_t(x, t, mean, var):
    return pl.pallas_call(
        fine_t_kernel,
        grid=(STRIPS[0] // CHUNK,),
        out_shape=jax.ShapeDtypeStruct((1, 80, COLS[0]), f32),
        in_specs=both_specs(80, 0) + both_specs(80, 0) + [chunk_spec(64, 0)] * 2,
        out_specs=pl.BlockSpec((1, 80, 128 * CHUNK), lambda g: (0, 0, g)),
        scratch_shapes=[
            pltpu.VMEM((256, 256), bf16),
            pltpu.VMEM((6, 80, 128), f32),
            pltpu.VMEM((CHUNK + 1, 192, 128), bf16),
            pltpu.VMEM((CHUNK + 1, 192, 128), bf16),
        ],
        compiler_params=PARAMS,
        cost_estimate=cost(8),
        name="fine_t",
    )(x, x, t, t, mean, var)


def ends(rows, last):
    return [
        pl.BlockSpec((STRIPS[0], rows, 128), lambda g: (0, 0, 0)),
        pl.BlockSpec((STRIPS[0], rows, 128), lambda g: (0, last, 0)),
    ]


def rest_x(xs, low, high):
    shapes = [jax.ShapeDtypeStruct((TILES[k], WORK[k] if k else 16, 128), f32) for k in range(5)]
    out = pl.pallas_call(
        rest_x_kernel,
        grid=(1,),
        out_shape=shapes * 2,
        in_specs=[VMEM] * 6 + ends(16, 4),
        out_specs=[VMEM] * 10,
        scratch_shapes=[
            pltpu.VMEM((256, 256), bf16),
            pltpu.VMEM((256, 128), bf16),
            pltpu.VMEM((6, 64, 128), f32),
            pltpu.VMEM((36, 96, 128), bf16),
            pltpu.VMEM((36, 96, 128), bf16),
            pltpu.VMEM((10, 64, 128), bf16),
        ],
        compiler_params=PARAMS,
        cost_estimate=cost(5),
        name="rest_x",
    )(*xs[1:], low, high, xs[0], xs[0])
    return out


def rest(xs, ts, edges, stats, fine):
    shapes = [jax.ShapeDtypeStruct((1, 80, COLS[0]), f32), jax.ShapeDtypeStruct((1, 40, COLS[1]), f32)]
    shapes += [jax.ShapeDtypeStruct((ROWS[k], 1, COLS[k]), f32) for k in range(2, 5)]
    fine, half, *small = pl.pallas_call(
        rest_kernel,
        grid=(1,),
        out_shape=shapes,
        in_specs=[VMEM] * 22 + ends(16, 4) * 2 + [ANYWHERE],
        out_specs=[ANYWHERE] + [VMEM] * 4,
        input_output_aliases={26: 0},
        scratch_shapes=[
            pltpu.VMEM((256, 256), bf16),
            pltpu.VMEM((256, 128), bf16),
            pltpu.VMEM((9, 64, 128), f32),
            pltpu.VMEM((36, 144, 128), bf16),
            pltpu.VMEM((36, 144, 128), bf16),
            pltpu.VMEM((10, 96, 128), bf16),
            pltpu.VMEM((2, 8, COLS[0]), f32),
            pltpu.SemaphoreType.DMA((2,)),
        ],
        compiler_params=pltpu.CompilerParams(vmem_limit_bytes=24 * 1024 * 1024),
        name="rest",
    )(*xs[1:], *ts[1:], *edges, *stats, xs[0], xs[0], ts[0], ts[0], fine)
    return (fine, half) + tuple(value.transpose(1, 0, 2) for value in small)


def local(samples, truth_field):
    forward = [(i, i + 1) for i in range(7)]
    backward = [(i + 1, i) for i in range(7)]
    prepare = functools.partial(
        pl.pallas_call,
        out_shape=level_shapes(),
        in_specs=[VMEM],
        out_specs=[VMEM] * 7,
        scratch_shapes=[pltpu.VMEM((256, 128), bf16)],
        compiler_params=PARAMS,
        cost_estimate=cost(4),
    )
    packed = pl.pallas_call(
        pack_kernel,
        out_shape=jax.ShapeDtypeStruct((88, 128), f32),
        in_specs=[VMEM],
        out_specs=VMEM,
        compiler_params=PARAMS,
        name="pack",
    )(truth_field.T)
    near = along_z(packed, 1)
    three, two = join([packed, near, along_z(packed, -1)], head=176)
    far = [along_z(three, 3), along_z(two, -3)]
    *xs, x_low, x_high = prepare(sample_kernel, name="samples")(samples)
    mean, var = fine_x(xs[0])
    (column,) = join([three, *far], mean)
    up, down = along_y(column, 1), along_y(column, -1)
    x_low = lax.ppermute(x_low, "rows", forward)
    x_high = lax.ppermute(x_high, "rows", backward)
    first, second = cut(up, down)
    far = [along_y(first, 1), along_y(second, -1)]
    stats = rest_x(xs, x_low, x_high)
    (whole,) = join([column, up, *far, down])
    *ts, low, high = prepare(truth_kernel, name="truth", in_specs=[VMEM, ANYWHERE])(whole, stats[4])
    low = lax.ppermute(low, "rows", forward)
    high = lax.ppermute(high, "rows", backward)
    fine = fine_t(xs[0], ts[0], mean, var)
    return rest(xs, ts, (x_low, x_high, low, high), stats, fine)


def solution(mesh):
    placed = (P("samp", "rows", None), P("rows", "samp"))
    return jax.shard_map(
        local,
        mesh=mesh,
        in_specs=placed,
        out_specs=(P("samp", "rows", None),) * 5,
        check_vma=False,
    )
```
